128 devices in a mesh: head: 4 (over y_lo, core), tile: 32 (over y_hi, z, x).
Axes of the slice: x: 4, y: 4 (y_hi: 2, y_lo: 2; y = y_hi * 2 + y_lo), z: 4, core: 2. Of those that a mesh axis runs over, the one named last changes fastest.
Arguments:
- queries: bfloat16 [64, 384, 3072], P('tile', 'head'), may hold values from -16 to 16
- keys: bfloat16 [64, 384, 3072], P('tile', 'head'), may hold values from -8 to 8
- values: bfloat16 [64, 384, 3072], P('tile', 'head'), may hold values from -6 to 6
- neighbours: int32 [64, 27], P('tile'), may hold values from -1 to 63, as said below
- w_out: bfloat16 [3072, 3072], P('head'), may hold values from -1.25 to 1.25
Outputs:
- projected: bfloat16 [64, 384, 3072], P('tile', 'head')
The draws below stay inside these ranges and needn't reach their ends.
Inputs may be any that keep to these rules, and one draw needn't show every extreme that they name: `neighbours`: tile s lies at time s % 2, height s // 2 // 8 and width s // 2 % 8 of a grid of 2 x 4 x 8 tiles. Entry j of row s is either -1 or the tile at offset (j // 9 - 1, j // 3 % 3 - 1, j % 3 - 1) from tile s in that grid; it is -1 where that tile lies outside the grid and may be -1 elsewhere too; entry 13 (the tile itself) is never -1.
All inputs are finite; a program needn't handle non-finite values.
Results may differ from the reference program's by a relative error of at most 0.017.
Values may be sent and summed in bfloat16 or wider, within the bound.
No kernel may reach another device: no remote copies, remote signals or barrier semaphores. Data moves between devices by JAX's collectives and lax.ppermute only.
A program may use at most 192 MiB of HBM per device.

```python
import jax
import jax.numpy as jnp
from jax import lax

D = 3072
HEADS = 24
HEAD_DIM = 128
TILE_TOK = 384
NEIGH = 27
TT = 2
DEV_H = 4
NTILES = 64


def draw_queries(key, part):
    key = jax.random.fold_in(key, 1)
    full_shape = (NTILES, TILE_TOK, D)
    return (1.41 * jax.random.truncated_normal(key, -4.0, 4.0, full_shape, jnp.float32)).astype(jnp.bfloat16)


def draw_keys(key, part):
    key = jax.random.fold_in(key, 2)
    full_shape = (NTILES, TILE_TOK, D)
    return (1.41 * jax.random.truncated_normal(key, -4.0, 4.0, full_shape, jnp.float32)).astype(jnp.bfloat16)


def draw_neighbours(key, part):
    key = jax.random.fold_in(key, 5)
    grid_width = NTILES // TT // DEV_H
    tile_index = jnp.arange(NTILES, dtype=jnp.int32)[:, None]
    offset = jnp.arange(NEIGH, dtype=jnp.int32)[None, :]
    owner = tile_index // TT
    time_next = tile_index % TT + offset // 9 - 1
    row_next = owner // grid_width + offset // 3 % 3 - 1
    column_next = owner % grid_width + offset % 3 - 1
    inside = (time_next >= 0) & (time_next < TT) & (row_next >= 0) & (row_next < DEV_H)
    inside = inside & (column_next >= 0) & (column_next < grid_width)
    kept_entry = jax.random.randint(key, (NTILES, NEIGH), 0, 4) > 0
    kept_entry = kept_entry | (offset == 13)
    target = (row_next * grid_width + column_next) * TT + time_next
    return jnp.where(inside & kept_entry, target, -1).astype(jnp.int32)


def levels(rng, extent, pieces, smallest, largest):
    factor_of = 1.0
    for axis_at, parts in pieces:
        heights = jax.random.uniform(jax.random.fold_in(jax.random.fold_in(rng, 6), axis_at), (parts,), jnp.float32, smallest / len(pieces), largest / len(pieces))
        factor_of = factor_of * jnp.repeat(jnp.exp(heights), extent[axis_at] // parts).reshape((-1,) + (1,) * (len(extent) - 1 - axis_at))
    return factor_of


def gaussian(rng, extent, deviation, reach, shards=(), kind=jnp.bfloat16):
    values = jax.random.normal(rng, extent, jnp.float32) * deviation
    if len(shards) > 0:
        values = levels(rng, extent, shards, -0.22, 0.18) * values
    return jnp.clip(values, min=-reach, max=reach).astype(kind)


def setup_inputs(seed: int = 0) -> dict:
    key_list = jax.random.split(jax.random.key(seed), 6)
    queries = draw_queries(jax.random.fold_in(key_list[5], 71), 0)
    keys = draw_keys(jax.random.fold_in(key_list[5], 71), 0)
    values = gaussian(key_list[2], (NTILES, TILE_TOK, D), 1.0, 6.0, ((0, 32), (1, 4)))
    neighbours = draw_neighbours(jax.random.fold_in(key_list[5], 71), 0)
    w_out = gaussian(key_list[4], (D, D), (max(D // 128, 1)) ** -0.5, 1.25, ((0, 4),))
    return dict(queries=queries, keys=keys, values=values, neighbours=neighbours, w_out=w_out)


def reference(queries, keys, values, neighbours, w_out):
    score_scale = HEAD_DIM ** -0.5

    def attend_tile(operands):
        query_block, tile_list = operands
        present = tile_list >= 0
        safe_list = jnp.where(present, tile_list, 0).astype(jnp.int32)
        key_rows = keys[safe_list].reshape(NEIGH * TILE_TOK, HEADS, HEAD_DIM).astype(jnp.float32)
        value_rows = values[safe_list].reshape(NEIGH * TILE_TOK, HEADS, HEAD_DIM).astype(jnp.float32)
        query_rows = query_block.reshape(TILE_TOK, HEADS, HEAD_DIM).astype(jnp.float32)
        scores = jnp.einsum("qhd,khd->qhk", query_rows, key_rows, precision=lax.Precision.HIGHEST) * score_scale
        key_mask = jnp.repeat(present, TILE_TOK)[None, None, :]
        scores = jnp.where(key_mask, scores, jnp.float32(-1e30))
        row_max = jnp.max(scores, axis=2, keepdims=True)
        weights = jnp.where(key_mask, jnp.exp(scores - row_max), jnp.float32(0.0))
        row_sum = jnp.sum(weights, axis=2)
        probs = weights.astype(jnp.bfloat16).astype(jnp.float32)
        weighted = jnp.einsum("qhk,khd->qhd", probs, value_rows, precision=lax.Precision.HIGHEST)
        return (weighted / row_sum[:, :, None]).astype(jnp.bfloat16).reshape(TILE_TOK, D)

    attention = lax.map(attend_tile, (queries, neighbours))
    flat_rows = attention.reshape(NTILES * TILE_TOK, D)
    projected = jnp.dot(flat_rows, w_out, preferred_element_type=jnp.float32)
    return projected.astype(jnp.bfloat16).reshape(NTILES, TILE_TOK, D)
```

```python
import functools

import jax
import jax.numpy as jnp
from jax import lax
from jax.experimental import pallas as pl
from jax.experimental.pallas import tpu as pltpu
from jax.sharding import Mesh, PartitionSpec as P

HEAD_DIM = 128
HEADS = 24
GROUPS = 8
GROUP_HEADS = HEADS // GROUPS
ROWS = 4
COLUMNS = 8
TIMES = 2
PART = 96
D = HEADS * HEAD_DIM
NEIGH = 27
COEF = HEAD_DIM ** (-0.5) * 1.4426950408889634
LOW = -1e30
CHUNKS = ((0, 1, 2),)

AXES = ("yl", "c", "yh", "zh", "zl", "x")
SIZES = (2, 2, 2, 2, 2, 4)
COLUMN_AXES = ("yh", "zh", "yl")


def places():
    for flat in range(128):
        left, coords = flat, []
        for size in reversed(SIZES):
            coords.append(left % size)
            left //= size
        yield flat, tuple(reversed(coords))


def flat_of(coords):
    flat = 0
    for coord, size in zip(coords, SIZES):
        flat = flat * size + coord
    return flat


def route(target):
    pairs = []
    for flat, coords in places():
        to = target(*coords)
        if to is not None:
            pairs.append((flat, flat_of(to)))
    return pairs


def column_step(step):
    def target(yl, c, yh, zh, zl, x):
        column = zl * 4 + x + step
        if not 0 <= column < COLUMNS:
            return None
        return (yl, c, yh, zh, column // 4, column % 4)

    return target


def y_step(step):
    def target(yl, c, yh, zh, zl, x):
        y = (yh * 2 + yl + step) % 4
        return (y % 2, c, y // 2, zh, zl, x)

    return target


RIGHT = route(column_step(1))
LEFT = route(column_step(-1))
UP = route(y_step(1))
DOWN = route(y_step(-1))
OTHER_CORE = route(lambda yl, c, yh, zh, zl, x: (yl, 1 - c, yh, zh, zl, x))


def permute(array, pairs):
    return lax.ppermute(array, AXES, pairs)


def exchange(array):
    return lax.all_to_all(array, COLUMN_AXES, 0, 0)


def arrange_kernel(q_ref, k_ref, v_ref, *out_refs):
    for at, chunk in enumerate(CHUNKS):
        q_out, kv_out = out_refs[2 * at], out_refs[2 * at + 1]
        lanes = pl.ds(chunk[0] * HEAD_DIM, len(chunk) * HEAD_DIM)
        q_out[0] = q_ref[:, :, lanes]
        kv_out[0, 0] = k_ref[:, :, lanes]
        kv_out[0, 1] = v_ref[:, :, lanes]


def arrange(queries, keys, values):
    shapes, specs = [], []
    for chunk in CHUNKS:
        width = len(chunk) * HEAD_DIM
        shapes.append(jax.ShapeDtypeStruct((GROUPS, TIMES, PART, width), jnp.bfloat16))
        specs.append(pl.BlockSpec((1, TIMES, PART, width), lambda g: (g, 0, 0, 0)))
        shapes.append(jax.ShapeDtypeStruct((GROUPS, 2, TIMES, PART, width), jnp.bfloat16))
        specs.append(pl.BlockSpec((1, 2, TIMES, PART, width), lambda g: (g, 0, 0, 0, 0)))
    block = pl.BlockSpec((TIMES, PART, GROUP_HEADS * HEAD_DIM), lambda g: (0, 0, g))
    return pl.pallas_call(
        arrange_kernel,
        grid=(GROUPS,),
        in_specs=[block] * 3,
        out_specs=specs,
        out_shape=shapes,
        name="arrange",
    )(queries, keys, values)


def attend_kernel(lists, q_ref, *refs):
    kv_refs, o_ref = refs[:6], refs[6]
    m_ref, l_ref, acc_ref = refs[7:]
    row = pl.program_id(1)
    half = 2 * PART
    q = jnp.concatenate([q_ref[:, t].reshape(half, HEAD_DIM) for t in range(TIMES)], axis=0)
    m_ref[...] = jnp.full(m_ref.shape, LOW, jnp.float32)
    l_ref[...] = jnp.zeros(l_ref.shape, jnp.float32)
    acc_ref[...] = jnp.zeros(acc_ref.shape, jnp.float32)

    def flag(t, t2, row_step, column_step):
        entry = (t2 - t + 1) * 9 + (row_step + 1) * 3 + column_step + 1
        return lists[(row * TIMES + t) * NEIGH + entry] >= 0

    for column in (0, -1, 1):
        own, other = kv_refs[2 * (column % 3)], kv_refs[2 * (column % 3) + 1]

        def step(index, carry, own=own, other=other, column=column):
            row_step = index - 1
            key_row = row + row_step
            flags = [[flag(t, t2, row_step, column) for t in range(TIMES)] for t2 in range(TIMES)]
            some = flags[0][0] | flags[0][1] | flags[1][0] | flags[1][1]

            @pl.when((key_row >= 0) & (key_row < ROWS) & some)
            def _():
                at = pl.ds(2 * key_row, 2)

                def tile(which, t2):
                    return [own[at, which, t2].reshape(half, HEAD_DIM), other[at, which, t2].reshape(half, HEAD_DIM)]

                k = jnp.concatenate(tile(0, 0) + tile(0, 1), axis=0)
                v = jnp.concatenate(tile(1, 0) + tile(1, 1), axis=0)
                s = lax.dot_general(q, k, (((1,), (1,)), ((), ())), preferred_element_type=jnp.float32)
                keys = 4 * PART
                m_old = m_ref[...]
                tops, shifts = [], []
                for t in range(TIMES):
                    best = m_old[t * half : (t + 1) * half, :1]
                    for t2 in range(TIMES):
                        part = s[t * half : (t + 1) * half, t2 * keys : (t2 + 1) * keys]
                        top = jnp.max(part, axis=1, keepdims=True)
                        best = jnp.maximum(best, jnp.where(flags[t2][t], top, LOW))
                    tops.append(best)
                m_new = jnp.concatenate(tops, axis=0)
                probs = []
                for t2 in range(TIMES):
                    shift = jnp.concatenate(
                        [jnp.where(flags[t2][t], tops[t] * COEF, -LOW) for t in range(TIMES)], axis=0
                    )
                    probs.append(jnp.exp2(s[:, t2 * keys : (t2 + 1) * keys] * COEF - shift))
                p = jnp.concatenate(probs, axis=1)
                factor = jnp.exp2((m_old - m_new) * COEF)
                total = p[:, :HEAD_DIM]
                for lane in range(1, p.shape[1] // HEAD_DIM):
                    total = total + p[:, lane * HEAD_DIM : (lane + 1) * HEAD_DIM]
                l_ref[...] = l_ref[...] * factor + total
                update = jnp.dot(p.astype(jnp.bfloat16), v, preferred_element_type=jnp.float32)
                acc_ref[...] = acc_ref[...] * factor + update
                m_ref[...] = jnp.broadcast_to(m_new, m_ref.shape)

            return carry

        lax.fori_loop(0, 3, step, 0)
    row_sum = jnp.sum(l_ref[...], axis=1, keepdims=True)
    out = (acc_ref[...] / row_sum).astype(jnp.bfloat16)
    for t in range(TIMES):
        o_ref[:, t] = out[t * half : (t + 1) * half].reshape(2, PART, HEAD_DIM)


def attend(lists, q, blocks):
    heads = q.shape[-1] // HEAD_DIM
    q_spec = pl.BlockSpec((2, TIMES, PART, HEAD_DIM), lambda h, r, s: (r, 0, 0, h))
    kv_spec = pl.BlockSpec((GROUPS, 2, TIMES, PART, HEAD_DIM), lambda h, r, s: (0, 0, 0, 0, h))
    tile_rows = 4 * PART
    return pl.pallas_call(
        attend_kernel,
        grid_spec=pltpu.PrefetchScalarGridSpec(
            num_scalar_prefetch=1,
            grid=(heads, ROWS),
            in_specs=[q_spec] + [kv_spec] * 6,
            out_specs=q_spec,
            scratch_shapes=[pltpu.VMEM((tile_rows, HEAD_DIM), jnp.float32)] * 3,
        ),
        out_shape=jax.ShapeDtypeStruct(q.shape, jnp.bfloat16),
        compiler_params=pltpu.CompilerParams(vmem_limit_bytes=40 * 1024 * 1024),
        cost_estimate=pl.CostEstimate(
            flops=heads * 30 * 384 * 768 * 128 * 4,
            bytes_accessed=heads * 6 * 786432,
            transcendentals=heads * 30 * 384 * 768,
        ),
        name="attend",
    )(lists, q, *blocks)


def project_kernel(ids, *refs):
    att_refs = refs[: len(CHUNKS)]
    w_refs, o_ref = refs[len(CHUNKS) : -1], refs[-1]
    total = None
    for shard in range(4):
        for part in range(2):
            group = ids[shard] * 2 + part
            rows = jnp.concatenate(
                [ref[group].reshape(TIMES * PART, ref.shape[-1]) for ref in att_refs], axis=1
            )
            w = w_refs[2 * shard + part][...]
            term = jnp.dot(rows, w, preferred_element_type=jnp.float32)
            total = term if total is None else total + term
    o_ref[...] = total.astype(jnp.bfloat16).reshape(TIMES, PART, total.shape[1])


def project(ids, parts, w_own, w_other, w_above, w_below, w_above_other, w_below_other):
    block = 512
    group_rows = D // GROUPS
    specs = []
    for part in parts:
        specs.append(pl.BlockSpec(part.shape, lambda n, s: (0, 0, 0, 0)))
    first = pl.BlockSpec((group_rows, block), lambda n, s: (0, n))
    second = pl.BlockSpec((group_rows, block), lambda n, s: (1, n))
    specs += [first, second, first, second, first, first, first, first]
    return pl.pallas_call(
        project_kernel,
        grid_spec=pltpu.PrefetchScalarGridSpec(
            num_scalar_prefetch=1,
            grid=(D // block,),
            in_specs=specs,
            out_specs=pl.BlockSpec((TIMES, PART, block), lambda n, s: (0, 0, n)),
        ),
        out_shape=jax.ShapeDtypeStruct((TIMES, PART, D), jnp.bfloat16),
        compiler_params=pltpu.CompilerParams(vmem_limit_bytes=40 * 1024 * 1024),
        cost_estimate=pl.CostEstimate(
            flops=2 * TIMES * PART * D * D, bytes_accessed=2 * D * D, transcendentals=0
        ),
        name="project",
    )(ids, *parts, w_own, w_own, w_other, w_other, w_above, w_below, w_above_other, w_below_other)


def on_device(queries, keys, values, neighbours, w_out):
    lists = lax.all_gather(neighbours, ("yh", "zh")).reshape(-1)
    arranged = arrange(queries, keys, values)
    results = []
    half = w_out.shape[0] // 2
    w_above = permute(w_out[:half], DOWN)
    w_below = permute(w_out[half:], UP)
    w_other = permute(w_out, OTHER_CORE)
    w_above_other = permute(w_above, OTHER_CORE)
    w_below_other = permute(w_below, OTHER_CORE)
    for at in range(len(CHUNKS)):
        kv = exchange(arranged[2 * at + 1])
        from_left = permute(kv, RIGHT)
        from_right = permute(kv, LEFT)
        q = exchange(arranged[2 * at])
        blocks = []
        for block in (kv, from_right, from_left):
            blocks += [block, permute(block, OTHER_CORE)]
        results.append(exchange(attend(lists, q, blocks)))
    yl, c = lax.axis_index("yl"), lax.axis_index("c")
    ids = jnp.stack([2 * yl + c, 2 * yl + 1 - c, 2 * (1 - yl) + c, 2 * (1 - yl) + 1 - c]).astype(jnp.int32)
    return project(ids, results, w_out, w_other, w_above, w_below, w_above_other, w_below_other)


def solution(mesh):
    fine = Mesh(mesh.devices.reshape(SIZES), AXES)
    tile, head = ("yh", "zh", "zl", "x"), ("yl", "c")
    placed = (
        P(tile, head, None),
        P(tile, head, None),
        P(tile, head, None),
        P(tile, None),
        P(head, None),
    )
    return jax.shard_map(
        on_device, mesh=fine, in_specs=placed, out_specs=P(tile, head, None), check_vma=False
    )
```

```python
import functools

import jax
import jax.numpy as jnp
from jax import lax
from jax.experimental import pallas as pl
from jax.experimental.pallas import tpu as pltpu
from jax.sharding import Mesh, PartitionSpec as P

HEAD_DIM = 128
HEADS = 24
GROUPS = 8
GROUP_HEADS = HEADS // GROUPS
ROWS = 4
COLUMNS = 8
TIMES = 2
PART = 96
D = HEADS * HEAD_DIM
NEIGH = 27
COEF = HEAD_DIM ** (-0.5) * 1.4426950408889634
LOW = -1e30
TILE = 4 * PART
CELL = TIMES * TILE
PAIRS = 10
PARTS = ((0,), (1, 2))
Q_AT = 1

AXES = ("yl", "c", "yh", "zh", "zl", "x")
SIZES = (2, 2, 2, 2, 2, 4)
COLUMN_AXES = ("yh", "zh", "yl")


def places():
    for flat in range(128):
        left, coords = flat, []
        for size in reversed(SIZES):
            coords.append(left % size)
            left //= size
        yield flat, tuple(reversed(coords))


def flat_of(coords):
    flat = 0
    for coord, size in zip(coords, SIZES):
        flat = flat * size + coord
    return flat


def route(target):
    pairs = []
    for flat, coords in places():
        to = target(*coords)
        if to is not None:
            pairs.append((flat, flat_of(to)))
    return pairs


def column_step(step):
    def target(yl, c, yh, zh, zl, x):
        column = zl * 4 + x + step
        if not 0 <= column < COLUMNS:
            return None
        return (yl, c, yh, zh, column // 4, column % 4)

    return target


def y_step(step):
    def target(yl, c, yh, zh, zl, x):
        y = (yh * 2 + yl + step) % 4
        return (y % 2, c, y // 2, zh, zl, x)

    return target


RIGHT = route(column_step(1))
LEFT = route(column_step(-1))
FAR = route(lambda yl, c, yh, zh, zl, x: y_step(1 if c else -1)(yl, c, yh, zh, zl, x))
FLIP_Z = route(lambda yl, c, yh, zh, zl, x: (yl, c, yh, 1 - zh, zl, x))
FLIP_Y = route(lambda yl, c, yh, zh, zl, x: (yl, c, 1 - yh, zh, zl, x))
FLIP_BOTH = route(lambda yl, c, yh, zh, zl, x: (yl, c, 1 - yh, 1 - zh, zl, x))
OTHER_CORE = route(lambda yl, c, yh, zh, zl, x: (yl, 1 - c, yh, zh, zl, x))


def permute(array, pairs):
    return lax.ppermute(array, AXES, pairs)


def exchange(array):
    return lax.all_to_all(array, COLUMN_AXES, 0, 0)


def arrange(*arrays):
    ins, outs, shapes, count = [], [], [], []
    for stack, heads in arrays:
        lanes = len(heads) * HEAD_DIM
        inner = (TIMES, PART, lanes) if len(stack) == 1 else (len(stack), TIMES, PART, lanes)
        shapes.append(jax.ShapeDtypeStruct((GROUPS,) + inner, jnp.bfloat16))
        outs.append(pl.BlockSpec((1,) + inner, lambda g, size=len(inner): (g,) + (0,) * size))
        for array in stack:
            ins.append(array)
        count.append((len(stack), heads))

    def kernel(*refs):
        at = 0
        for out_ref, (size, heads) in zip(refs[len(ins) :], count):
            lanes = pl.ds(heads[0] * HEAD_DIM, len(heads) * HEAD_DIM)
            for which in range(size):
                value = refs[at][:, :, lanes]
                if size == 1:
                    out_ref[0] = value
                else:
                    out_ref[0, which] = value
                at += 1

    block = pl.BlockSpec((TIMES, PART, GROUP_HEADS * HEAD_DIM), lambda g: (0, 0, g))
    return pl.pallas_call(
        kernel,
        grid=(GROUPS,),
        in_specs=[block] * len(ins),
        out_specs=outs,
        out_shape=shapes,
        compiler_params=pltpu.CompilerParams(vmem_limit_bytes=58 * 1024 * 1024),
        name="arrange",
    )(*ins)


def attend_kernel(plan, lists, q_ref, *refs):
    units, slots, sources, taken, given, done, passed = plan
    pass_refs, refs = refs[:passed], refs[passed:]
    kv_refs, refs = refs[:sources], refs[sources:]
    state_in, refs = refs[: 3 * taken], refs[3 * taken :]
    o_refs, refs = refs[:done], refs[done:]
    state_out, refs = refs[: 3 * given], refs[3 * given :]
    kv_ref, vt_ref, qt_ref, m_ref, l_ref, acc_ref, s_refs, p_refs, top_refs, factor_refs, sems = refs
    half = 2 * PART

    def load(unit, core):
        slot, column, pair, lane = units[unit]
        source = kv_refs[pair[core]].at[:, :, :, :, pl.ds(lane * HEAD_DIM, HEAD_DIM)]
        return pltpu.make_async_copy(source, kv_ref.at[unit, core], sems.at[unit, core])

    for unit in range(len(units)):
        for core in range(2):
            load(unit, core).start()

    fresh = 0
    for slot, (lane, begin, end) in enumerate(slots):
        mine = pl.ds(slot * ROWS, ROWS)
        if begin is None:
            m_ref[mine] = jnp.full((ROWS, 1, TILE), LOW, jnp.float32)
            l_ref[mine] = jnp.zeros((ROWS, 8, TILE), jnp.float32)
            acc_ref[mine] = jnp.zeros((ROWS, HEAD_DIM, TILE), jnp.float32)
        else:
            for at, ref in enumerate((m_ref, l_ref, acc_ref)):
                ref[mine] = state_in[3 * begin + at][...]
        for row in range(ROWS):
            lanes = slice(lane * HEAD_DIM, (lane + 1) * HEAD_DIM)
            q = [q_ref[2 * row : 2 * row + 2, t, :, lanes].reshape(half, HEAD_DIM) for t in range(TIMES)]
            qt_ref[slot * ROWS + row] = jnp.concatenate(q, axis=0).T
    for at, ref in enumerate(pass_refs):
        o_refs[0][:, :, :, at * HEAD_DIM : (at + 1) * HEAD_DIM] = ref[...]
    factor_refs[1][...] = jnp.ones(factor_refs[1].shape, jnp.float32)
    p_refs[1][...] = jnp.zeros(p_refs[1].shape, jnp.bfloat16)
    first = lax.broadcasted_iota(jnp.int32, (1, TILE), 1) < half

    def choose(unit, values):
        result = jnp.int32(values[0])
        for at in range(1, len(values)):
            result = jnp.where(unit >= at, jnp.int32(values[at]), result)
        return result

    slot_of = [unit[0] for unit in units]
    column_of = [unit[1] + 1 for unit in units]

    def cell(which, unit, key_row):
        parts = []
        for t2 in range(TIMES):
            for core in range(2):
                for yl in range(2):
                    parts.append(kv_ref[unit, core, 2 * key_row + yl, which, t2])
        return jnp.concatenate(parts, axis=0)

    def turn(unit):
        def body(key_row, carry):
            vt_ref[unit * ROWS + key_row] = cell(1, unit, key_row).T
            return carry

        lax.fori_loop(0, ROWS, body, 0)

    def place(at):
        at = jnp.clip(at, 0, len(units) * PAIRS - 1)
        unit, spot = at // PAIRS, at % PAIRS + 1
        row, step = spot // 3, spot % 3
        return unit, row, row + step - 1, step

    def score(at, s_ref, top_ref):
        unit, row, key_row, step = place(at)
        qt = qt_ref[choose(unit, slot_of) * ROWS + row]
        s = jnp.dot(cell(0, unit, key_row), qt, preferred_element_type=jnp.float32)
        s_ref[...] = s
        for t2 in range(TIMES):
            top_ref[t2] = jnp.max(s[t2 * TILE : (t2 + 1) * TILE].reshape(TILE // 8, 8, TILE), axis=0)

    def weigh(at, s_ref, top_ref, p_ref, factor_ref):
        unit, row, key_row, step = place(at)
        spot = choose(unit, slot_of) * ROWS + row
        start = (lists[ROWS * TIMES * NEIGH] ^ row) * (TIMES * NEIGH) + step * 3 + choose(unit, column_of)
        oks = []
        for t2 in range(TIMES):
            use = [lists[start + t * NEIGH + (t2 - t + 1) * 9] for t in range(TIMES)]
            oks.append(jnp.where(first, use[0], use[1]) >= 0)
        m_old = m_ref[spot]
        best = m_old
        for t2 in range(TIMES):
            top = jnp.max(top_ref[t2], axis=0, keepdims=True)
            best = jnp.maximum(best, jnp.where(oks[t2], top, LOW))
        m_ref[spot] = best
        factor = jnp.exp2((m_old - best) * COEF)
        factor_ref[...] = factor
        l = l_ref[spot] * factor
        shifts = [jnp.where(ok, best * COEF, -LOW) for ok in oks]
        for piece in range(6):
            rows = slice(piece * 128, (piece + 1) * 128)
            p = jnp.exp2(s_ref[rows] * COEF - shifts[piece // 3])
            l = l + jnp.sum(p.reshape(16, 8, TILE), axis=0)
            p_ref[rows] = p.astype(jnp.bfloat16)
        l_ref[spot] = l

    def absorb(at, p_ref, factor_ref):
        unit, row, key_row, step = place(at)
        spot = choose(unit, slot_of) * ROWS + row
        update = jnp.dot(vt_ref[unit * ROWS + key_row], p_ref[...], preferred_element_type=jnp.float32)
        acc_ref[spot] = acc_ref[spot] * factor_ref[...] + update

    for core in range(2):
        load(0, core).wait()
    turn(0)
    score(0, s_refs[0], top_refs[0])
    rounds = PAIRS // 2

    def round_of(index, carry):
        at = 2 * index
        for unit in range(1, len(units)):

            @pl.when(index == rounds * unit - 1)
            def _(unit=unit):
                for core in range(2):
                    load(unit, core).wait()

        @pl.when((index % rounds == rounds - 1) & (index < rounds * len(units) - 1))
        def _():
            turn(index // rounds + 1)

        score(at + 1, s_refs[1], top_refs[1])
        absorb(at - 1, p_refs[1], factor_refs[1])
        weigh(at, s_refs[0], top_refs[0], p_refs[0], factor_refs[0])
        score(at + 2, s_refs[0], top_refs[0])
        absorb(at, p_refs[0], factor_refs[0])
        weigh(at + 1, s_refs[1], top_refs[1], p_refs[1], factor_refs[1])
        return carry

    lax.fori_loop(0, rounds * len(units), round_of, 0)
    absorb(len(units) * PAIRS - 1, p_refs[1], factor_refs[1])
    for slot, (lane, begin, end) in enumerate(slots):
        if end[0] == "state":
            for at, ref in enumerate((m_ref, l_ref, acc_ref)):
                state_out[3 * end[1] + at][...] = ref[pl.ds(slot * ROWS, ROWS)]
            continue
        for row in range(ROWS):
            spot = slot * ROWS + row
            out = (acc_ref[spot] / jnp.sum(l_ref[spot], axis=0, keepdims=True)).T.astype(jnp.bfloat16)
            lanes = slice(end[2] * HEAD_DIM, (end[2] + 1) * HEAD_DIM)
            for t in range(TIMES):
                o_refs[end[1]][2 * row : 2 * row + 2, t, :, lanes] = out[t * half : (t + 1) * half].reshape(
                    2, PART, HEAD_DIM
                )


def attend(lists, q, blocks, units, slots, states, passed):
    given = sum(1 for slot in slots if slot[2][0] == "state")
    widths = {0: len(passed) * HEAD_DIM}
    for slot in slots:
        if slot[2][0] == "out":
            widths[slot[2][1]] = widths.get(slot[2][1], 0) + HEAD_DIM
    state_shapes = [(ROWS, 1, TILE), (ROWS, 8, TILE), (ROWS, HEAD_DIM, TILE)]
    shapes = [jax.ShapeDtypeStruct((GROUPS, TIMES, PART, widths[at]), jnp.bfloat16) for at in range(len(widths))]
    shapes += [jax.ShapeDtypeStruct(shape, jnp.float32) for shape in state_shapes] * given
    vmem, anywhere = pl.BlockSpec(memory_space=pltpu.VMEM), pl.BlockSpec(memory_space=pl.ANY)
    plan = (units, slots, len(blocks), len(states) // 3, given, len(widths), len(passed))
    count, spots = len(units), len(slots) * ROWS
    return pl.pallas_call(
        functools.partial(attend_kernel, plan),
        in_specs=[pl.BlockSpec(memory_space=pltpu.SMEM), vmem] + [vmem] * len(passed) + [anywhere] * len(blocks) + [vmem] * len(states),
        out_specs=[vmem] * len(shapes),
        scratch_shapes=[
            pltpu.VMEM((count, 2, GROUPS, 2, TIMES, PART, HEAD_DIM), jnp.bfloat16),
            pltpu.VMEM((count * ROWS, HEAD_DIM, CELL), jnp.bfloat16),
            pltpu.VMEM((spots, HEAD_DIM, TILE), jnp.bfloat16),
            pltpu.VMEM((spots, 1, TILE), jnp.float32),
            pltpu.VMEM((spots, 8, TILE), jnp.float32),
            pltpu.VMEM((spots, HEAD_DIM, TILE), jnp.float32),
            [pltpu.VMEM((CELL, TILE), jnp.float32)] * 2,
            [pltpu.VMEM((CELL, TILE), jnp.bfloat16)] * 2,
            [pltpu.VMEM((2, 8, TILE), jnp.float32)] * 2,
            [pltpu.VMEM((1, TILE), jnp.float32)] * 2,
            pltpu.SemaphoreType.DMA((count, 2)),
        ],
        out_shape=shapes,
        compiler_params=pltpu.CompilerParams(vmem_limit_bytes=58 * 1024 * 1024),
        cost_estimate=pl.CostEstimate(
            flops=count * PAIRS * 384 * 768 * 128 * 4,
            bytes_accessed=count * 2 * 786432,
            transcendentals=count * PAIRS * 384 * 768,
        ),
        name="attend",
    )(lists, q, *passed, *blocks, *states)


def project_kernel(ids, att_ref, *refs):
    w_refs, o_ref = refs[:-1], refs[-1]
    total = None
    for shard in range(4):
        for part in range(2):
            rows = att_ref[ids[shard] * 2 + part].reshape(TIMES * PART, GROUP_HEADS * HEAD_DIM)
            term = jnp.dot(rows, w_refs[2 * shard + part][...], preferred_element_type=jnp.float32)
            total = term if total is None else total + term
    o_ref[...] = total.astype(jnp.bfloat16).reshape(TIMES, PART, total.shape[1])


def project(ids, att, *shards):
    block = 512
    rows = D // GROUPS
    specs, pieces = [pl.BlockSpec(att.shape, lambda n, s: (0, 0, 0, 0))], []
    for shard in shards:
        for part in range(2):
            specs.append(pl.BlockSpec((rows, block), lambda n, s, part=part: (part, n)))
            pieces.append(shard)
    return pl.pallas_call(
        project_kernel,
        grid_spec=pltpu.PrefetchScalarGridSpec(
            num_scalar_prefetch=1,
            grid=(D // block,),
            in_specs=specs,
            out_specs=pl.BlockSpec((TIMES, PART, block), lambda n, s: (0, 0, n)),
        ),
        out_shape=jax.ShapeDtypeStruct((TIMES, PART, D), jnp.bfloat16),
        compiler_params=pltpu.CompilerParams(vmem_limit_bytes=58 * 1024 * 1024),
        cost_estimate=pl.CostEstimate(
            flops=2 * TIMES * PART * D * D, bytes_accessed=2 * D * D, transcendentals=0
        ),
        name="project",
    )(ids, att, *pieces)


def on_device(queries, keys, values, neighbours, w_out):
    live = {"w": w_out, "near": neighbours, "qkv": (queries, keys, values)}

    def fence():
        names = list(live)
        for name, value in zip(names, lax.optimization_barrier([live[name] for name in names])):
            live[name] = value

    def sides(at):
        kv = live["kv", at]
        live["left", at], live["right", at] = permute(kv, RIGHT), permute(kv, LEFT)

    def swap(*names):
        for name, at in names:
            live[name + "_other", at] = permute(live[name, at], OTHER_CORE)

    def work(units, slots, states, passed):
        blocks, spots, found = [], {}, []
        for slot, column, name, at, lane in units:
            for end in (name, name + "_other"):
                if (end, at) not in spots:
                    spots[end, at] = len(blocks)
                    blocks.append(live[end, at])
            found.append((slot, column, (spots[name, at], spots[name + "_other", at]), lane))
        return attend(live["lists"], live["q"], blocks, tuple(found), tuple(slots), states, passed)

    (live["part", 0],) = arrange(((keys, values), PARTS[0]))
    fence()
    queries, keys, values = live.pop("qkv")
    live["kv", 0] = exchange(live.pop(("part", 0)))
    live["part", 1], q_part = arrange(((keys, values), PARTS[1]), ((queries,), range(GROUP_HEADS)))
    if Q_AT == 0:
        live["q"] = exchange(q_part)
    else:
        live["q_part"] = q_part
    row = lax.axis_index("yh") * 2 + lax.axis_index("zh")
    flips = [live["near"].reshape(-1)]
    for pairs in (FLIP_Z, FLIP_Y, FLIP_BOTH):
        flips.append(permute(live["near"], pairs).reshape(-1))
    live["lists"] = jnp.concatenate(flips + [row.astype(jnp.int32).reshape(1)])
    live["w_other", 0] = permute(live["w"], OTHER_CORE)
    fence()
    live["kv", 1] = exchange(live.pop(("part", 1)))
    if Q_AT == 1:
        live["q"] = exchange(live.pop("q_part"))
    sides(0)
    swap(("kv", 0))
    fence()
    if Q_AT == 2:
        live["q"] = exchange(live.pop("q_part"))
    sides(1)
    swap(("kv", 1), ("left", 0), ("right", 0))
    live["far", 0] = permute(live["w"], FAR)
    units = [(0, 0, "kv", 0, 0), (1, 0, "kv", 1, 0), (2, 0, "kv", 1, 1), (0, -1, "left", 0, 0), (0, 1, "right", 0, 0)]
    slots = [(0, None, ("out", 0, 0)), (1, None, ("state", 0)), (2, None, ("state", 1))]
    done, *states = work(units, slots, [], [])
    live["done"] = done
    for at, state in enumerate(states):
        live["state", at] = state
    fence()
    swap(("left", 1), ("right", 1))
    fence()
    swap(("far", 0))
    units = [(0, -1, "left", 1, 0), (1, -1, "left", 1, 1), (0, 1, "right", 1, 0), (1, 1, "right", 1, 1)]
    slots = [(1, 0, ("out", 0, 1)), (2, 1, ("out", 0, 2))]
    (live["att"],) = work(units, slots, [live.pop(("state", at)) for at in range(6)], [live.pop("done")])
    fence()
    att = exchange(live["att"])
    yl, c = lax.axis_index("yl"), lax.axis_index("c")
    ids = jnp.stack([2 * yl + c, 2 * yl + 1 - c, 2 * (1 - yl) + c, 2 * (1 - yl) + 1 - c]).astype(jnp.int32)
    return project(ids, att, live["w"], live["w_other", 0], live["far", 0], live["far_other", 0])


def solution(mesh):
    fine = Mesh(mesh.devices.reshape(SIZES), AXES)
    tile, head = ("yh", "zh", "zl", "x"), ("yl", "c")
    placed = (
        P(tile, head, None),
        P(tile, head, None),
        P(tile, head, None),
        P(tile, None),
        P(head, None),
    )
    return jax.shard_map(
        on_device, mesh=fine, in_specs=placed, out_specs=P(tile, head, None), check_vma=False
    )
```

```python
import functools

import jax
import jax.numpy as jnp
from jax import lax
from jax.experimental import pallas as pl
from jax.experimental.pallas import tpu as pltpu
from jax.sharding import Mesh, PartitionSpec as P

HEAD_DIM = 128
HEADS = 24
GROUPS = 8
GROUP_HEADS = HEADS // GROUPS
ROWS = 4
COLUMNS = 8
TIMES = 2
PART = 96
D = HEADS * HEAD_DIM
NEIGH = 27
COEF = HEAD_DIM ** (-0.5) * 1.4426950408889634
LOW = -1e30
TILE = 4 * PART
CELL = TIMES * TILE
PAIRS = 10
ALL = tuple(range(GROUP_HEADS))
QUARTER = 2 * PART
ATT_VMEM = 32
PROJ_VMEM = 58

AXES = ("yl", "c", "yh", "zh", "zl", "x")
SIZES = (2, 2, 2, 2, 2, 4)
COLUMN_AXES = ("yh", "zh", "yl")


def places():
    for flat in range(128):
        left, coords = flat, []
        for size in reversed(SIZES):
            coords.append(left % size)
            left //= size
        yield flat, tuple(reversed(coords))


def flat_of(coords):
    flat = 0
    for coord, size in zip(coords, SIZES):
        flat = flat * size + coord
    return flat


def route(target):
    pairs = []
    for flat, coords in places():
        to = target(*coords)
        if to is not None:
            pairs.append((flat, flat_of(to)))
    return pairs


def column_step(step):
    def target(yl, c, yh, zh, zl, x):
        column = zl * 4 + x + step
        if not 0 <= column < COLUMNS:
            return None
        return (yl, c, yh, zh, column // 4, column % 4)

    return target


def y_step(step):
    def target(yl, c, yh, zh, zl, x):
        y = (yh * 2 + yl + step) % 4
        return (y % 2, c, y // 2, zh, zl, x)

    return target


RIGHT = route(column_step(1))
LEFT = route(column_step(-1))
FAR = route(lambda yl, c, yh, zh, zl, x: y_step(1 if c else -1)(yl, c, yh, zh, zl, x))
FLIP_Z = route(lambda yl, c, yh, zh, zl, x: (yl, c, yh, 1 - zh, zl, x))
FLIP_Y = route(lambda yl, c, yh, zh, zl, x: (yl, c, 1 - yh, zh, zl, x))
FLIP_BOTH = route(lambda yl, c, yh, zh, zl, x: (yl, c, 1 - yh, 1 - zh, zl, x))
OTHER_CORE = route(lambda yl, c, yh, zh, zl, x: (yl, 1 - c, yh, zh, zl, x))


def permute(array, pairs):
    return lax.ppermute(array, AXES, pairs)


def exchange(array):
    return lax.all_to_all(array, COLUMN_AXES, 0, 0)


def arrange(*arrays):
    ins, outs, shapes, count = [], [], [], []
    for stack, heads in arrays:
        lanes = len(heads) * HEAD_DIM
        inner = (TIMES, PART, lanes) if len(stack) == 1 else (len(stack), TIMES, PART, lanes)
        shapes.append(jax.ShapeDtypeStruct((GROUPS,) + inner, jnp.bfloat16))
        outs.append(pl.BlockSpec((1,) + inner, lambda g, size=len(inner): (g,) + (0,) * size))
        for array in stack:
            ins.append(array)
        count.append((len(stack), heads))

    def kernel(*refs):
        at = 0
        for out_ref, (size, heads) in zip(refs[len(ins) :], count):
            lanes = pl.ds(heads[0] * HEAD_DIM, len(heads) * HEAD_DIM)
            for which in range(size):
                value = refs[at][:, :, lanes]
                if size == 1:
                    out_ref[0] = value
                else:
                    out_ref[0, which] = value
                at += 1

    block = pl.BlockSpec((TIMES, PART, GROUP_HEADS * HEAD_DIM), lambda g: (0, 0, g))
    return pl.pallas_call(
        kernel,
        grid=(GROUPS,),
        in_specs=[block] * len(ins),
        out_specs=outs,
        out_shape=shapes,
        compiler_params=pltpu.CompilerParams(vmem_limit_bytes=58 * 1024 * 1024),
        name="arrange",
    )(*ins)


def attend_kernel(plan, lists, q_ref, *refs):
    sides, taken, last = plan
    kv_refs, refs = refs[:2], refs[2:]
    state_in, refs = refs[:taken], refs[taken:]
    if last:
        o_ref, m_ref, l_ref, acc_ref = refs[:4]
    else:
        m_ref, l_ref, acc_ref = refs[:3]
    kv_ref, vt_ref, qt_ref, s_refs, p_refs, top_refs, factor_refs, sems = refs[-8:]
    heads = kv_ref.shape[0]

    def load(head, which):
        lanes = pl.ds(head * HEAD_DIM, HEAD_DIM)
        return [
            pltpu.make_async_copy(
                kv_refs[side].at[:, which, :, :, lanes], kv_ref.at[head, which, side], sems.at[head, which, side]
            )
            for side in range(2)
        ]

    for head in range(heads):
        for which in range(2):
            for copy in load(head, which):
                copy.start()

    if taken:
        for ref, given in zip((m_ref, l_ref, acc_ref), state_in):
            ref[...] = given[...]
    else:
        m_ref[...] = jnp.full(m_ref.shape, LOW, jnp.float32)
        l_ref[...] = jnp.zeros(l_ref.shape, jnp.float32)
        acc_ref[...] = jnp.zeros(acc_ref.shape, jnp.float32)
    for head in range(heads):
        lanes = slice(head * HEAD_DIM, (head + 1) * HEAD_DIM)
        for row in range(ROWS):
            q = [q_ref[2 * row : 2 * row + 2, t, :, lanes].reshape(QUARTER, HEAD_DIM) for t in range(TIMES)]
            qt_ref[head * ROWS + row] = jnp.concatenate(q, axis=0).T
    for part in range(2):
        factor_refs[part][...] = jnp.ones(factor_refs[part].shape, jnp.float32)
        p_refs[part][...] = jnp.zeros(p_refs[part].shape, jnp.bfloat16)
    first = lax.broadcasted_iota(jnp.int32, (1, TILE), 1) < QUARTER

    def cell(which, head, key_row):
        parts = []
        for side in range(2):
            for t2 in range(TIMES):
                for yl in range(2):
                    parts.append(kv_ref[head, which, side, 2 * key_row + yl, t2])
        return jnp.concatenate(parts, axis=0)

    def turn(head):
        def body(key_row, carry):
            vt_ref[head * ROWS + key_row] = cell(1, head, key_row).T
            return carry

        lax.fori_loop(0, ROWS, body, 0)

    def place(at):
        row, step = (at + 1) // 3, (at + 1) % 3
        return row, row + step - 1, step

    def score(head, at):
        row, key_row, step = place(at)
        s_ref, top_ref = s_refs[at % 2], top_refs[at % 2]
        s = jnp.dot(cell(0, head, key_row), qt_ref[head * ROWS + row], preferred_element_type=jnp.float32)
        s_ref[...] = s
        for part in range(4):
            rows = s[part * QUARTER : (part + 1) * QUARTER]
            top_ref[part] = jnp.max(rows.reshape(QUARTER // 8, 8, TILE), axis=0)

    def weigh(head, at):
        row, key_row, step = place(at)
        s_ref, top_ref, p_ref = s_refs[at % 2], top_refs[at % 2], p_refs[at % 2]
        spot = head * ROWS + row
        start = (lists[ROWS * TIMES * NEIGH] ^ row) * (TIMES * NEIGH) + step * 3
        oks = []
        for side in range(2):
            for t2 in range(TIMES):
                entry = start + (sides[side] + 1)
                use = [lists[entry + (t * NEIGH + (t2 - t + 1) * 9)] for t in range(TIMES)]
                oks.append(jnp.where(first, use[0], use[1]) >= 0)
        m_old = m_ref[spot]
        best = m_old
        for part in range(4):
            top = jnp.max(top_ref[part], axis=0, keepdims=True)
            best = jnp.maximum(best, jnp.where(oks[part], top, LOW))
        m_ref[spot] = best
        factor = jnp.exp2((m_old - best) * COEF)
        factor_refs[at % 2][...] = factor
        l = l_ref[spot] * factor
        shifts = [jnp.where(ok, best * COEF, -LOW) for ok in oks]
        for piece in range(8):
            rows = slice(piece * PART, (piece + 1) * PART)
            p = jnp.exp2(s_ref[rows] * COEF - shifts[piece // 2])
            l = l + jnp.sum(p.reshape(PART // 8, 8, TILE), axis=0)
            p_ref[rows] = p.astype(jnp.bfloat16)
        l_ref[spot] = l

    def absorb(head, at):
        row, key_row, step = place(at)
        spot = head * ROWS + row
        update = jnp.dot(vt_ref[head * ROWS + key_row], p_refs[at % 2][...], preferred_element_type=jnp.float32)
        acc_ref[spot] = acc_ref[spot] * factor_refs[at % 2][...] + update

    for copy in load(0, 0):
        copy.wait()
    score(0, 0)
    score(0, 1)

    def per_head(index, carry):
        for head in range(heads):

            @pl.when(index == head)
            def _(head=head):
                for copy in load(head, 1):
                    copy.wait()
                if head + 1 < heads:
                    for copy in load(head + 1, 0):
                        copy.wait()

        turn(index)
        before, following = jnp.maximum(index - 1, 0), jnp.minimum(index + 1, heads - 1)
        for at in range(PAIRS):
            if at < 2:
                absorb(before, at + PAIRS - 2)
            else:
                absorb(index, at - 2)
            weigh(index, at)
            if at + 2 < PAIRS:
                score(index, at + 2)
            else:
                score(following, at + 2 - PAIRS)
        return carry

    lax.fori_loop(0, heads, per_head, 0)
    absorb(heads - 1, PAIRS - 2)
    absorb(heads - 1, PAIRS - 1)
    if last:
        for head in range(heads):
            lanes = slice(head * HEAD_DIM, (head + 1) * HEAD_DIM)
            for row in range(ROWS):
                spot = head * ROWS + row
                out = (acc_ref[spot] / jnp.sum(l_ref[spot], axis=0, keepdims=True)).T.astype(jnp.bfloat16)
                for t in range(TIMES):
                    rows = out[t * QUARTER : (t + 1) * QUARTER].reshape(2, PART, HEAD_DIM)
                    o_ref[2 * row : 2 * row + 2, t, :, lanes] = rows


def attend(lists, q, blocks, sides, state=(), last=False):
    heads = q.shape[-1] // HEAD_DIM
    spots = heads * ROWS
    state_shapes = [(spots, 1, TILE), (spots, 8, TILE), (spots, HEAD_DIM, TILE)]
    vmem, anywhere = pl.BlockSpec(memory_space=pltpu.VMEM), pl.BlockSpec(memory_space=pl.ANY)
    scratch = []
    if last:
        shapes = [jax.ShapeDtypeStruct(q.shape, jnp.bfloat16)]
        scratch = [pltpu.VMEM(shape, jnp.float32) for shape in state_shapes]
    else:
        shapes = [jax.ShapeDtypeStruct(shape, jnp.float32) for shape in state_shapes]
    return pl.pallas_call(
        functools.partial(attend_kernel, (sides, len(state), last)),
        in_specs=[pl.BlockSpec(memory_space=pltpu.SMEM), vmem] + [anywhere] * 2 + [vmem] * len(state),
        out_specs=[vmem] * len(shapes),
        scratch_shapes=scratch
        + [
            pltpu.VMEM((heads, 2, 2, GROUPS, TIMES, PART, HEAD_DIM), jnp.bfloat16),
            pltpu.VMEM((spots, HEAD_DIM, CELL), jnp.bfloat16),
            pltpu.VMEM((spots, HEAD_DIM, TILE), jnp.bfloat16),
            [pltpu.VMEM((CELL, TILE), jnp.float32)] * 2,
            [pltpu.VMEM((CELL, TILE), jnp.bfloat16)] * 2,
            [pltpu.VMEM((4, 8, TILE), jnp.float32)] * 2,
            [pltpu.VMEM((1, TILE), jnp.float32)] * 2,
            pltpu.SemaphoreType.DMA((heads, 2, 2)),
        ],
        out_shape=shapes,
        compiler_params=pltpu.CompilerParams(vmem_limit_bytes=ATT_VMEM * 1024 * 1024),
        cost_estimate=pl.CostEstimate(
            flops=heads * PAIRS * 384 * 768 * 128 * 4,
            bytes_accessed=heads * 2 * 786432,
            transcendentals=heads * PAIRS * 384 * 768,
        ),
        name="attend",
    )(lists, q, *blocks, *state)


def project_kernel(ids, att_ref, *refs):
    w_refs, o_ref = refs[:-1], refs[-1]
    total = None
    for shard in range(4):
        for part in range(2):
            rows = att_ref[ids[shard] * 2 + part].reshape(TIMES * PART, GROUP_HEADS * HEAD_DIM)
            term = jnp.dot(rows, w_refs[2 * shard + part][...], preferred_element_type=jnp.float32)
            total = term if total is None else total + term
    o_ref[...] = total.astype(jnp.bfloat16).reshape(TIMES, PART, total.shape[1])


def project(ids, att, *shards):
    block = 512
    rows = D // GROUPS
    specs, pieces = [pl.BlockSpec(att.shape, lambda n, s: (0, 0, 0, 0))], []
    for shard in shards:
        for part in range(2):
            specs.append(pl.BlockSpec((rows, block), lambda n, s, part=part: (part, n)))
            pieces.append(shard)
    return pl.pallas_call(
        project_kernel,
        grid_spec=pltpu.PrefetchScalarGridSpec(
            num_scalar_prefetch=1,
            grid=(D // block,),
            in_specs=specs,
            out_specs=pl.BlockSpec((TIMES, PART, block), lambda n, s: (0, 0, n)),
        ),
        out_shape=jax.ShapeDtypeStruct((TIMES, PART, D), jnp.bfloat16),
        compiler_params=pltpu.CompilerParams(vmem_limit_bytes=PROJ_VMEM * 1024 * 1024),
        cost_estimate=pl.CostEstimate(
            flops=2 * TIMES * PART * D * D, bytes_accessed=2 * D * D, transcendentals=0
        ),
        name="project",
    )(ids, att, *pieces)


def on_device(queries, keys, values, neighbours, w_out):
    live = {"w": w_out, "near": neighbours, "queries": queries, "keys": keys, "values": values}

    def fence():
        names = list(live)
        for name, value in zip(names, lax.optimization_barrier([live[name] for name in names])):
            live[name] = value

    def swap(name):
        live[name + "_other"] = permute(live[name], OTHER_CORE)

    def work(left, right, state=(), last=False):
        blocks = [live[left[0]], live[right[0]]]
        return attend(live["lists"], live["q"], blocks, (left[1], right[1]), state, last)

    (live["q"],) = arrange(((live.pop("queries"),), ALL))
    fence()
    live["q"] = exchange(live["q"])
    (live["kv"],) = arrange(((live.pop("keys"), live.pop("values")), ALL))
    row = lax.axis_index("yh") * 2 + lax.axis_index("zh")
    flips = [live["near"].reshape(-1)]
    for pairs in (FLIP_Z, FLIP_Y, FLIP_BOTH):
        flips.append(permute(live["near"], pairs).reshape(-1))
    live["lists"] = jnp.concatenate(flips + [row.astype(jnp.int32).reshape(1)])
    fence()
    live["kv"] = exchange(live["kv"])
    swap("w")
    fence()
    live["left"], live["right"] = permute(live["kv"], RIGHT), permute(live["kv"], LEFT)
    swap("kv")
    live["far"] = permute(live["w"], FAR)
    state = work(("kv", 0), ("kv_other", 0))
    for at in range(3):
        live["state", at] = state[at]
    fence()
    swap("left")
    swap("right")
    state = work(("left", -1), ("right", 1), [live.pop(("state", at)) for at in range(3)])
    for at in range(3):
        live["state", at] = state[at]
    fence()
    swap("far")
    (live["att"],) = work(("left_other", -1), ("right_other", 1), [live.pop(("state", at)) for at in range(3)], True)
    fence()
    att = exchange(live["att"])
    yl, c = lax.axis_index("yl"), lax.axis_index("c")
    ids = jnp.stack([2 * yl + c, 2 * yl + 1 - c, 2 * (1 - yl) + c, 2 * (1 - yl) + 1 - c]).astype(jnp.int32)
    return project(ids, att, live["w"], live["w_other"], live["far"], live["far_other"])


def solution(mesh):
    fine = Mesh(mesh.devices.reshape(SIZES), AXES)
    tile, head = ("yh", "zh", "zl", "x"), ("yl", "c")
    placed = (
        P(tile, head, None),
        P(tile, head, None),
        P(tile, head, None),
        P(tile, None),
        P(head, None),
    )
    return jax.shard_map(
        on_device, mesh=fine, in_specs=placed, out_specs=P(tile, head, None), check_vma=False
    )
```

```python
import functools

import jax
import jax.numpy as jnp
from jax import lax
from jax.experimental import pallas as pl
from jax.experimental.pallas import tpu as pltpu
from jax.sharding import Mesh, PartitionSpec as P

HEAD_DIM = 128
HEADS = 24
GROUPS = 8
GROUP_HEADS = HEADS // GROUPS
ROWS = 4
COLUMNS = 8
TIMES = 2
PART = 96
D = HEADS * HEAD_DIM
NEIGH = 27
COEF = HEAD_DIM ** (-0.5) * 1.4426950408889634
LOW = -1e30
TILE = 4 * PART
CELL = TIMES * TILE
PAIRS = 10
QUARTER = 2 * PART
ATT_VMEM = 24
PROJ_VMEM = 58
ARRANGE_VMEM = 8

AXES = ("yl", "c", "yh", "zh", "zl", "x")
SIZES = (2, 2, 2, 2, 2, 4)
COLUMN_AXES = ("yh", "zh", "yl")


def places():
    for flat in range(128):
        left, coords = flat, []
        for size in reversed(SIZES):
            coords.append(left % size)
            left //= size
        yield flat, tuple(reversed(coords))


def flat_of(coords):
    flat = 0
    for coord, size in zip(coords, SIZES):
        flat = flat * size + coord
    return flat


def route(target):
    pairs = []
    for flat, coords in places():
        to = target(*coords)
        if to is not None:
            pairs.append((flat, flat_of(to)))
    return pairs


def column_step(step):
    def target(yl, c, yh, zh, zl, x):
        column = zl * 4 + x + step
        if not 0 <= column < COLUMNS:
            return None
        return (yl, c, yh, zh, column // 4, column % 4)

    return target


def y_step(step):
    def target(yl, c, yh, zh, zl, x):
        y = (yh * 2 + yl + step) % 4
        return (y % 2, c, y // 2, zh, zl, x)

    return target


RIGHT = route(column_step(1))
LEFT = route(column_step(-1))
FAR = route(lambda yl, c, yh, zh, zl, x: y_step(1 if c else -1)(yl, c, yh, zh, zl, x))
FLIP_Z = route(lambda yl, c, yh, zh, zl, x: (yl, c, yh, 1 - zh, zl, x))
FLIP_Y = route(lambda yl, c, yh, zh, zl, x: (yl, c, 1 - yh, zh, zl, x))
FLIP_BOTH = route(lambda yl, c, yh, zh, zl, x: (yl, c, 1 - yh, 1 - zh, zl, x))
OTHER_CORE = route(lambda yl, c, yh, zh, zl, x: (yl, 1 - c, yh, zh, zl, x))


def permute(array, pairs):
    return lax.ppermute(array, AXES, pairs)


def exchange(array):
    return lax.all_to_all(array, COLUMN_AXES, 0, 0)


def arrange_kernel(stack, *refs):
    in_refs, out_ref, sems = refs[:stack], refs[stack], refs[stack + 1]
    copies = []
    for g in range(GROUPS):
        lanes = pl.ds(g * GROUP_HEADS * HEAD_DIM, GROUP_HEADS * HEAD_DIM)
        for at, ref in enumerate(in_refs):
            to = out_ref.at[g] if stack == 1 else out_ref.at[g, at]
            copies.append(pltpu.make_async_copy(ref.at[:, :, lanes], to, sems.at[g, at]))
    for copy in copies:
        copy.start()
    for copy in copies:
        copy.wait()


def arrange(*stack):
    inner = (TIMES, PART, GROUP_HEADS * HEAD_DIM)
    shape = (GROUPS,) + (inner if len(stack) == 1 else (len(stack),) + inner)
    return pl.pallas_call(
        functools.partial(arrange_kernel, len(stack)),
        in_specs=[pl.BlockSpec(memory_space=pl.ANY)] * len(stack),
        out_specs=pl.BlockSpec(memory_space=pltpu.VMEM),
        scratch_shapes=[pltpu.SemaphoreType.DMA((GROUPS, len(stack)))],
        out_shape=jax.ShapeDtypeStruct(shape, jnp.bfloat16),
        compiler_params=pltpu.CompilerParams(vmem_limit_bytes=ARRANGE_VMEM * 1024 * 1024),
        name="arrange",
    )(*stack)


def attend_kernel(plan, mine, *refs):
    sides, taken, last = plan
    near_refs, q_ref, refs = refs[:ROWS], refs[ROWS], refs[ROWS + 1 :]
    lists, refs = refs[-1], refs[:-1]
    for flip, near in enumerate(near_refs):
        start = (mine[0] ^ flip) * (TIMES * NEIGH)
        for t in range(TIMES):
            for entry in range(NEIGH):
                lists[start + (t * NEIGH + entry)] = near[t, entry]
    kv_refs, refs = refs[:2], refs[2:]
    state_in, refs = refs[:taken], refs[taken:]
    if last:
        o_ref, m_ref, l_ref, acc_ref = refs[:4]
    else:
        m_ref, l_ref, acc_ref = refs[:3]
    vt_ref, qt_ref, s_refs, p_refs, top_refs, factor_refs = refs[-6:]
    heads = q_ref.shape[-1] // HEAD_DIM

    if taken:
        for ref, given in zip((m_ref, l_ref, acc_ref), state_in):
            ref[...] = given[...]
    else:
        m_ref[...] = jnp.full(m_ref.shape, LOW, jnp.float32)
        l_ref[...] = jnp.zeros(l_ref.shape, jnp.float32)
        acc_ref[...] = jnp.zeros(acc_ref.shape, jnp.float32)
    for head in range(heads):
        lanes = slice(head * HEAD_DIM, (head + 1) * HEAD_DIM)
        for row in range(ROWS):
            q = [q_ref[2 * row : 2 * row + 2, t, :, lanes].reshape(QUARTER, HEAD_DIM) for t in range(TIMES)]
            qt_ref[head * ROWS + row] = jnp.concatenate(q, axis=0).T
    for part in range(2):
        factor_refs[part][...] = jnp.ones(factor_refs[part].shape, jnp.float32)
        p_refs[part][...] = jnp.zeros(p_refs[part].shape, jnp.bfloat16)
    first = lax.broadcasted_iota(jnp.int32, (1, TILE), 1) < QUARTER

    def cell(which, head, key_row):
        parts = []
        lanes = pl.ds(pl.multiple_of(head * HEAD_DIM, HEAD_DIM), HEAD_DIM)
        for side in range(2):
            for t2 in range(TIMES):
                for yl in range(2):
                    parts.append(kv_refs[side][2 * key_row + yl, which, t2, :, lanes])
        return jnp.concatenate(parts, axis=0)

    def turn(head):
        def body(key_row, carry):
            vt_ref[head * ROWS + key_row] = cell(1, head, key_row).T
            return carry

        lax.fori_loop(0, ROWS, body, 0)

    def place(at):
        row, step = (at + 1) // 3, (at + 1) % 3
        return row, row + step - 1, step

    def score(head, at):
        row, key_row, step = place(at)
        s_ref, top_ref = s_refs[at % 2], top_refs[at % 2]
        s = jnp.dot(cell(0, head, key_row), qt_ref[head * ROWS + row], preferred_element_type=jnp.float32)
        s_ref[...] = s
        for part in range(4):
            rows = s[part * QUARTER : (part + 1) * QUARTER]
            top_ref[part] = jnp.max(rows.reshape(QUARTER // 8, 8, TILE), axis=0)

    def weigh(head, at):
        row, key_row, step = place(at)
        s_ref, top_ref, p_ref = s_refs[at % 2], top_refs[at % 2], p_refs[at % 2]
        spot = head * ROWS + row
        start = row * TIMES * NEIGH + step * 3
        oks = []
        for side in range(2):
            for t2 in range(TIMES):
                entry = start + sides[side] + 1
                use = [lists[entry + t * NEIGH + (t2 - t + 1) * 9] for t in range(TIMES)]
                oks.append(jnp.where(first, use[0], use[1]) >= 0)
        m_old = m_ref[spot]
        best = m_old
        for part in range(4):
            top = jnp.max(top_ref[part], axis=0, keepdims=True)
            best = jnp.maximum(best, jnp.where(oks[part], top, LOW))
        m_ref[spot] = best
        factor = jnp.exp2((m_old - best) * COEF)
        factor_refs[at % 2][...] = factor
        l = l_ref[spot] * factor
        shifts = [jnp.where(ok, best * COEF, -LOW) for ok in oks]
        for piece in range(8):
            rows = slice(piece * PART, (piece + 1) * PART)
            p = jnp.exp2(s_ref[rows] * COEF - shifts[piece // 2])
            l = l + jnp.sum(p.reshape(PART // 8, 8, TILE), axis=0)
            p_ref[rows] = p.astype(jnp.bfloat16)
        l_ref[spot] = l

    def absorb(head, at):
        row, key_row, step = place(at)
        spot = head * ROWS + row
        update = jnp.dot(vt_ref[head * ROWS + key_row], p_refs[at % 2][...], preferred_element_type=jnp.float32)
        acc_ref[spot] = acc_ref[spot] * factor_refs[at % 2][...] + update

    score(0, 0)
    score(0, 1)

    def per_head(index, carry):
        turn(index)
        before, following = jnp.maximum(index - 1, 0), jnp.minimum(index + 1, heads - 1)
        for at in range(PAIRS):
            if at < 2:
                absorb(before, at + PAIRS - 2)
            else:
                absorb(index, at - 2)
            weigh(index, at)
            if at + 2 < PAIRS:
                score(index, at + 2)
            else:
                score(following, at + 2 - PAIRS)
        return carry

    lax.fori_loop(0, heads, per_head, 0)
    absorb(heads - 1, PAIRS - 2)
    absorb(heads - 1, PAIRS - 1)
    if last:
        for head in range(heads):
            lanes = slice(head * HEAD_DIM, (head + 1) * HEAD_DIM)
            for row in range(ROWS):
                spot = head * ROWS + row
                out = (acc_ref[spot] / jnp.sum(l_ref[spot], axis=0, keepdims=True)).T.astype(jnp.bfloat16)
                for t in range(TIMES):
                    rows = out[t * QUARTER : (t + 1) * QUARTER].reshape(2, PART, HEAD_DIM)
                    o_ref[2 * row : 2 * row + 2, t, :, lanes] = rows


def attend(lists, q, blocks, sides, state=(), last=False):
    heads = q.shape[-1] // HEAD_DIM
    spots = heads * ROWS
    state_shapes = [(spots, 1, TILE), (spots, 8, TILE), (spots, HEAD_DIM, TILE)]
    vmem = pl.BlockSpec(memory_space=pltpu.VMEM)
    scratch = []
    if last:
        shapes = [jax.ShapeDtypeStruct(q.shape, jnp.bfloat16)]
        scratch = [pltpu.VMEM(shape, jnp.float32) for shape in state_shapes]
    else:
        shapes = [jax.ShapeDtypeStruct(shape, jnp.float32) for shape in state_shapes]
    return pl.pallas_call(
        functools.partial(attend_kernel, (sides, len(state), last)),
        in_specs=[pl.BlockSpec(memory_space=pltpu.SMEM)] * (1 + ROWS) + [vmem] * (3 + len(state)),
        out_specs=[vmem] * len(shapes),
        scratch_shapes=scratch
        + [
            pltpu.VMEM((spots, HEAD_DIM, CELL), jnp.bfloat16),
            pltpu.VMEM((spots, HEAD_DIM, TILE), jnp.bfloat16),
            [pltpu.VMEM((CELL, TILE), jnp.float32)] * 2,
            [pltpu.VMEM((CELL, TILE), jnp.bfloat16)] * 2,
            [pltpu.VMEM((4, 8, TILE), jnp.float32)] * 2,
            [pltpu.VMEM((1, TILE), jnp.float32)] * 2,
            pltpu.SMEM((ROWS * TIMES * NEIGH,), jnp.int32),
        ],
        out_shape=shapes,
        compiler_params=pltpu.CompilerParams(vmem_limit_bytes=ATT_VMEM * 1024 * 1024),
        cost_estimate=pl.CostEstimate(
            flops=heads * PAIRS * 384 * 768 * 128 * 4,
            bytes_accessed=heads * 2 * 786432,
            transcendentals=heads * PAIRS * 384 * 768,
        ),
        name="attend",
    )(*lists, q, *blocks, *state)


def project_kernel(ids, att_ref, *refs):
    w_refs, o_ref, w_ref, sum_ref, sems = refs[:4], refs[4], refs[5], refs[6], refs[7]
    rows = D // GROUPS
    copies = []
    for shard in range(4):
        for part in range(2):
            source = w_refs[shard].at[pl.ds(part * rows, rows)]
            at = 2 * shard + part
            copies.append(pltpu.make_async_copy(source, w_ref.at[at], sems.at[at]))
    for copy in copies:
        copy.start()
    block = 512
    for at, copy in enumerate(copies):
        copy.wait()
        left = att_ref[ids[at // 2] * 2 + at % 2].reshape(TIMES * PART, rows)
        for start in range(0, D, block):
            lanes = slice(start, start + block)
            term = jnp.dot(left, w_ref[at, :, lanes], preferred_element_type=jnp.float32)
            if at > 0:
                term = sum_ref[:, lanes] + term
            if at + 1 < len(copies):
                sum_ref[:, lanes] = term
            else:
                o_ref[:, :, lanes] = term.astype(jnp.bfloat16).reshape(TIMES, PART, block)


def project(ids, att, *shards):
    vmem, anywhere = pl.BlockSpec(memory_space=pltpu.VMEM), pl.BlockSpec(memory_space=pl.ANY)
    rows = D // GROUPS
    return pl.pallas_call(
        project_kernel,
        in_specs=[pl.BlockSpec(memory_space=pltpu.SMEM), vmem] + [anywhere] * len(shards),
        out_specs=vmem,
        scratch_shapes=[
            pltpu.VMEM((GROUPS, rows, D), jnp.bfloat16),
            pltpu.VMEM((TIMES * PART, D), jnp.float32),
            pltpu.SemaphoreType.DMA((GROUPS,)),
        ],
        out_shape=jax.ShapeDtypeStruct((TIMES, PART, D), jnp.bfloat16),
        compiler_params=pltpu.CompilerParams(vmem_limit_bytes=PROJ_VMEM * 1024 * 1024),
        cost_estimate=pl.CostEstimate(
            flops=2 * TIMES * PART * D * D, bytes_accessed=2 * D * D, transcendentals=0
        ),
        name="project",
    )(ids, att, *shards)


def on_device(queries, keys, values, neighbours, w_out):
    live = {"w": w_out, "near": neighbours, "queries": queries, "keys": keys, "values": values}

    def fence():
        live.update(lax.optimization_barrier(dict(live)))

    def swap(name):
        live[name + "_other"] = permute(live[name], OTHER_CORE)

    def work(left, right, state=(), last=False):
        blocks = [live[left[0]], live[right[0]]]
        return attend(live["lists"], live["q"], blocks, (left[1], right[1]), state, last)

    live["q"] = arrange(live.pop("queries"))
    fence()
    live["q"] = exchange(live["q"])
    live["kv"] = arrange(live.pop("keys"), live.pop("values"))
    near = live.pop("near")
    row = lax.axis_index("yh") * 2 + lax.axis_index("zh")
    lists = [row.astype(jnp.int32).reshape(1), near]
    for pairs in (FLIP_Z, FLIP_Y, FLIP_BOTH):
        lists.append(permute(near, pairs))
    live["lists"] = lists
    fence()
    live["kv"] = exchange(live["kv"])
    fence()
    live["left"], live["right"] = permute(live["kv"], RIGHT), permute(live["kv"], LEFT)
    swap("kv")
    late = lax.optimization_barrier((live["w"], live["kv_other"]))[0]
    far, w_other = permute(late, FAR), permute(late, OTHER_CORE)
    state = work(("kv", 0), ("kv_other", 0))
    for at in range(3):
        live["state%d" % at] = state[at]
    fence()
    swap("left")
    swap("right")
    state = work(("left", -1), ("right", 1), [live.pop("state%d" % at) for at in range(3)])
    for at in range(3):
        live["state%d" % at] = state[at]
    live["far"], live["w_other"] = far, w_other
    fence()
    swap("far")
    (live["att"],) = work(("left_other", -1), ("right_other", 1), [live.pop("state%d" % at) for at in range(3)], True)
    fence()
    att = exchange(live["att"])
    yl, c = lax.axis_index("yl"), lax.axis_index("c")
    ids = jnp.stack([2 * yl + c, 2 * yl + 1 - c, 2 * (1 - yl) + c, 2 * (1 - yl) + 1 - c]).astype(jnp.int32)
    return project(ids, att, live["w"], live["w_other"], live["far"], live["far_other"])


def solution(mesh):
    fine = Mesh(mesh.devices.reshape(SIZES), AXES)
    tile, head = ("yh", "zh", "zl", "x"), ("yl", "c")
    placed = (
        P(tile, head, None),
        P(tile, head, None),
        P(tile, head, None),
        P(tile, None),
        P(head, None),
    )
    return jax.shard_map(
        on_device, mesh=fine, in_specs=placed, out_specs=P(tile, head, None), check_vma=False
    )
```

```python
import functools

import jax
import jax.numpy as jnp
from jax import lax
from jax.experimental import pallas as pl
from jax.experimental.pallas import tpu as pltpu
from jax.sharding import Mesh, PartitionSpec as P

HEAD_DIM = 128
HEADS = 24
GROUPS = 8
GROUP_HEADS = HEADS // GROUPS
ROWS = 4
COLUMNS = 8
TIMES = 2
PART = 96
D = HEADS * HEAD_DIM
NEIGH = 27
COEF = HEAD_DIM ** (-0.5) * 1.4426950408889634
LOW = -1e30
TILE = 4 * PART
CELL = TIMES * TILE
PAIRS = 10
QUARTER = 2 * PART
ATT_VMEM = 24
PROJ_VMEM = 58
ARRANGE_VMEM = 8

AXES = ("yl", "c", "yh", "zh", "zl", "x")
SIZES = (2, 2, 2, 2, 2, 4)
COLUMN_AXES = ("yh", "zh", "yl")


def places():
    for flat in range(128):
        left, coords = flat, []
        for size in reversed(SIZES):
            coords.append(left % size)
            left //= size
        yield flat, tuple(reversed(coords))


def flat_of(coords):
    flat = 0
    for coord, size in zip(coords, SIZES):
        flat = flat * size + coord
    return flat


def route(target):
    pairs = []
    for flat, coords in places():
        to = target(*coords)
        if to is not None:
            pairs.append((flat, flat_of(to)))
    return pairs


def column_step(step):
    def target(yl, c, yh, zh, zl, x):
        column = zl * 4 + x + step
        if not 0 <= column < COLUMNS:
            return None
        return (yl, c, yh, zh, column // 4, column % 4)

    return target


def y_step(step):
    def target(yl, c, yh, zh, zl, x):
        y = (yh * 2 + yl + step) % 4
        return (y % 2, c, y // 2, zh, zl, x)

    return target


RIGHT = route(column_step(1))
LEFT = route(column_step(-1))
FAR = route(lambda yl, c, yh, zh, zl, x: y_step(1 if c else -1)(yl, c, yh, zh, zl, x))
FLIP_Z = route(lambda yl, c, yh, zh, zl, x: (yl, c, yh, 1 - zh, zl, x))
FLIP_Y = route(lambda yl, c, yh, zh, zl, x: (yl, c, 1 - yh, zh, zl, x))
FLIP_BOTH = route(lambda yl, c, yh, zh, zl, x: (yl, c, 1 - yh, 1 - zh, zl, x))
OTHER_CORE = route(lambda yl, c, yh, zh, zl, x: (yl, 1 - c, yh, zh, zl, x))


def permute(array, pairs):
    return lax.ppermute(array, AXES, pairs)


def exchange(array):
    return lax.all_to_all(array, COLUMN_AXES, 0, 0)


def arrange_kernel(stack, *refs):
    in_refs, out_ref, sems = refs[:stack], refs[stack], refs[stack + 1]
    copies = []
    for g in range(GROUPS):
        lanes = pl.ds(g * GROUP_HEADS * HEAD_DIM, GROUP_HEADS * HEAD_DIM)
        for at, ref in enumerate(in_refs):
            to = out_ref.at[g] if stack == 1 else out_ref.at[g, at]
            copies.append(pltpu.make_async_copy(ref.at[:, :, lanes], to, sems.at[g, at]))
    for copy in copies:
        copy.start()
    for copy in copies:
        copy.wait()


def arrange(*stack):
    inner = (TIMES, PART, GROUP_HEADS * HEAD_DIM)
    shape = (GROUPS,) + (inner if len(stack) == 1 else (len(stack),) + inner)
    return pl.pallas_call(
        functools.partial(arrange_kernel, len(stack)),
        in_specs=[pl.BlockSpec(memory_space=pl.ANY)] * len(stack),
        out_specs=pl.BlockSpec(memory_space=pltpu.VMEM),
        scratch_shapes=[pltpu.SemaphoreType.DMA((GROUPS, len(stack)))],
        out_shape=jax.ShapeDtypeStruct(shape, jnp.bfloat16),
        compiler_params=pltpu.CompilerParams(vmem_limit_bytes=ARRANGE_VMEM * 1024 * 1024),
        name="arrange",
    )(*stack)


def attend_kernel(plan, mine, *refs):
    sides, taken, last = plan
    near_refs, q_ref, refs = refs[:ROWS], refs[ROWS], refs[ROWS + 1 :]
    lists, refs = refs[-1], refs[:-1]
    for flip, near in enumerate(near_refs):
        start = (mine[0] ^ flip) * (TIMES * NEIGH)
        for t in range(TIMES):
            for entry in range(NEIGH):
                lists[start + (t * NEIGH + entry)] = near[t, entry]
    kv_refs, refs = refs[:2], refs[2:]
    state_in, refs = refs[:taken], refs[taken:]
    if last:
        o_ref, m_ref, l_ref, acc_ref = refs[:4]
    else:
        m_ref, l_ref, acc_ref = refs[:3]
    vt_ref, qt_ref, s_refs, p_refs, top_refs, factor_refs = refs[-6:]
    heads = q_ref.shape[-1] // HEAD_DIM

    if taken:
        for ref, given in zip((m_ref, l_ref, acc_ref), state_in):
            ref[...] = given[...]
    else:
        m_ref[...] = jnp.full(m_ref.shape, LOW, jnp.float32)
        l_ref[...] = jnp.zeros(l_ref.shape, jnp.float32)
        acc_ref[...] = jnp.zeros(acc_ref.shape, jnp.float32)
    for head in range(heads):
        lanes = slice(head * HEAD_DIM, (head + 1) * HEAD_DIM)
        for row in range(ROWS):
            q = [q_ref[2 * row : 2 * row + 2, t, :, lanes].reshape(QUARTER, HEAD_DIM) for t in range(TIMES)]
            qt_ref[head * ROWS + row] = jnp.concatenate(q, axis=0).T
    for part in range(2):
        factor_refs[part][...] = jnp.ones(factor_refs[part].shape, jnp.float32)
        p_refs[part][...] = jnp.zeros(p_refs[part].shape, jnp.bfloat16)
    first = lax.broadcasted_iota(jnp.int32, (1, TILE), 1) < QUARTER

    def cell(which, head, key_row):
        parts = []
        lanes = pl.ds(pl.multiple_of(head * HEAD_DIM, HEAD_DIM), HEAD_DIM)
        for side in range(2):
            for t2 in range(TIMES):
                for yl in range(2):
                    parts.append(kv_refs[side][2 * key_row + yl, which, t2, :, lanes])
        return jnp.concatenate(parts, axis=0)

    def turn(head):
        def body(key_row, carry):
            vt_ref[head * ROWS + key_row] = cell(1, head, key_row).T
            return carry

        lax.fori_loop(0, ROWS, body, 0)

    def place(at):
        row, step = (at + 1) // 3, (at + 1) % 3
        return row, row + step - 1, step

    def score(head, at):
        row, key_row, step = place(at)
        s_ref, top_ref = s_refs[at % 2], top_refs[at % 2]
        s = jnp.dot(cell(0, head, key_row), qt_ref[head * ROWS + row], preferred_element_type=jnp.float32)
        s_ref[...] = s
        for part in range(4):
            rows = s[part * QUARTER : (part + 1) * QUARTER]
            top_ref[part] = jnp.max(rows.reshape(QUARTER // 8, 8, TILE), axis=0)

    def weigh(head, at):
        row, key_row, step = place(at)
        s_ref, top_ref, p_ref = s_refs[at % 2], top_refs[at % 2], p_refs[at % 2]
        spot = head * ROWS + row
        start = row * TIMES * NEIGH + step * 3
        oks = []
        for side in range(2):
            for t2 in range(TIMES):
                entry = start + sides[side] + 1
                use = [lists[entry + t * NEIGH + (t2 - t + 1) * 9] for t in range(TIMES)]
                oks.append(jnp.where(first, use[0], use[1]) >= 0)
        m_old = m_ref[spot]
        best = m_old
        for part in range(4):
            top = jnp.max(top_ref[part], axis=0, keepdims=True)
            best = jnp.maximum(best, jnp.where(oks[part], top, LOW))
        m_ref[spot] = best
        factor = jnp.exp2((m_old - best) * COEF)
        factor_refs[at % 2][...] = factor
        l = l_ref[spot] * factor
        shifts = [jnp.where(ok, best * COEF, -LOW) for ok in oks]
        for piece in range(8):
            rows = slice(piece * PART, (piece + 1) * PART)
            p = jnp.exp2(s_ref[rows] * COEF - shifts[piece // 2])
            l = l + jnp.sum(p.reshape(PART // 8, 8, TILE), axis=0)
            p_ref[rows] = p.astype(jnp.bfloat16)
        l_ref[spot] = l

    def absorb(head, at):
        row, key_row, step = place(at)
        spot = head * ROWS + row
        update = jnp.dot(vt_ref[head * ROWS + key_row], p_refs[at % 2][...], preferred_element_type=jnp.float32)
        acc_ref[spot] = acc_ref[spot] * factor_refs[at % 2][...] + update

    score(0, 0)
    score(0, 1)

    def per_head(index, carry):
        turn(index)
        before, following = jnp.maximum(index - 1, 0), jnp.minimum(index + 1, heads - 1)
        for at in range(PAIRS):
            if at < 2:
                absorb(before, at + PAIRS - 2)
            else:
                absorb(index, at - 2)
            weigh(index, at)
            if at + 2 < PAIRS:
                score(index, at + 2)
            else:
                score(following, at + 2 - PAIRS)
        return carry

    lax.fori_loop(0, heads, per_head, 0)
    absorb(heads - 1, PAIRS - 2)
    absorb(heads - 1, PAIRS - 1)
    if last:
        for head in range(heads):
            lanes = slice(head * HEAD_DIM, (head + 1) * HEAD_DIM)
            for row in range(ROWS):
                spot = head * ROWS + row
                out = (acc_ref[spot] / jnp.sum(l_ref[spot], axis=0, keepdims=True)).T.astype(jnp.bfloat16)
                for t in range(TIMES):
                    rows = out[t * QUARTER : (t + 1) * QUARTER].reshape(2, PART, HEAD_DIM)
                    o_ref[2 * row : 2 * row + 2, t, :, lanes] = rows


def attend(lists, q, blocks, sides, state=(), last=False):
    heads = q.shape[-1] // HEAD_DIM
    spots = heads * ROWS
    state_shapes = [(spots, 1, TILE), (spots, 8, TILE), (spots, HEAD_DIM, TILE)]
    vmem = pl.BlockSpec(memory_space=pltpu.VMEM)
    scratch = []
    if last:
        shapes = [jax.ShapeDtypeStruct(q.shape, jnp.bfloat16)]
        scratch = [pltpu.VMEM(shape, jnp.float32) for shape in state_shapes]
    else:
        shapes = [jax.ShapeDtypeStruct(shape, jnp.float32) for shape in state_shapes]
    return pl.pallas_call(
        functools.partial(attend_kernel, (sides, len(state), last)),
        in_specs=[pl.BlockSpec(memory_space=pltpu.SMEM)] * (1 + ROWS) + [vmem] * (3 + len(state)),
        out_specs=[vmem] * len(shapes),
        scratch_shapes=scratch
        + [
            pltpu.VMEM((spots, HEAD_DIM, CELL), jnp.bfloat16),
            pltpu.VMEM((spots, HEAD_DIM, TILE), jnp.bfloat16),
            [pltpu.VMEM((CELL, TILE), jnp.float32)] * 2,
            [pltpu.VMEM((CELL, TILE), jnp.bfloat16)] * 2,
            [pltpu.VMEM((4, 8, TILE), jnp.float32)] * 2,
            [pltpu.VMEM((1, TILE), jnp.float32)] * 2,
            pltpu.SMEM((ROWS * TIMES * NEIGH,), jnp.int32),
        ],
        out_shape=shapes,
        compiler_params=pltpu.CompilerParams(vmem_limit_bytes=ATT_VMEM * 1024 * 1024),
        cost_estimate=pl.CostEstimate(
            flops=heads * PAIRS * 384 * 768 * 128 * 4,
            bytes_accessed=heads * 2 * 786432,
            transcendentals=heads * PAIRS * 384 * 768,
        ),
        name="attend",
    )(*lists, q, *blocks, *state)


def project_kernel(ids, att_in, *refs):
    w_refs, o_ref, att_ref, w_ref, sum_ref, out_ref, sems, out_sems = refs[:4], *refs[4:]
    rows = D // GROUPS
    bring = pltpu.make_async_copy(att_in, att_ref, sems.at[GROUPS])
    bring.start()
    copies = []
    for at in range(GROUPS):
        source = w_refs[at // 2].at[pl.ds(at % 2 * rows, rows)]
        copies.append(pltpu.make_async_copy(source, w_ref.at[at], sems.at[at]))
    ahead = 3
    for copy in copies[:ahead]:
        copy.start()
    bring.wait()
    block = 512
    results = []
    for at, copy in enumerate(copies):
        copy.wait()
        if at + ahead < GROUPS:
            copies[at + ahead].start()
        left = att_ref[ids[at // 2] * 2 + at % 2].reshape(TIMES * PART, rows)
        for start in range(0, D, block):
            lanes = slice(start, start + block)
            term = jnp.dot(left, w_ref[at, :, lanes], preferred_element_type=jnp.float32)
            if at > 0:
                term = sum_ref[:, lanes] + term
            if at + 1 < GROUPS:
                sum_ref[:, lanes] = term
            else:
                out_ref[:, :, lanes] = term.astype(jnp.bfloat16).reshape(TIMES, PART, block)
                spot = pl.ds(start, block)
                done = pltpu.make_async_copy(
                    out_ref.at[:, :, spot], o_ref.at[:, :, spot], out_sems.at[start // block]
                )
                done.start()
                results.append(done)
    for done in results:
        done.wait()


def project(ids, att, *shards):
    anywhere = pl.BlockSpec(memory_space=pl.ANY)
    rows = D // GROUPS
    return pl.pallas_call(
        project_kernel,
        in_specs=[pl.BlockSpec(memory_space=pltpu.SMEM)] + [anywhere] * (1 + len(shards)),
        out_specs=anywhere,
        scratch_shapes=[
            pltpu.VMEM(att.shape, jnp.bfloat16),
            pltpu.VMEM((GROUPS, rows, D), jnp.bfloat16),
            pltpu.VMEM((TIMES * PART, D), jnp.float32),
            pltpu.VMEM((TIMES, PART, D), jnp.bfloat16),
            pltpu.SemaphoreType.DMA((GROUPS + 1,)),
            pltpu.SemaphoreType.DMA((D // 512,)),
        ],
        out_shape=jax.ShapeDtypeStruct((TIMES, PART, D), jnp.bfloat16),
        compiler_params=pltpu.CompilerParams(vmem_limit_bytes=PROJ_VMEM * 1024 * 1024),
        cost_estimate=pl.CostEstimate(
            flops=2 * TIMES * PART * D * D, bytes_accessed=2 * D * D, transcendentals=0
        ),
        name="project",
    )(ids, att, *shards)


def on_device(queries, keys, values, neighbours, w_out):
    live = {"w": w_out, "near": neighbours, "queries": queries, "keys": keys, "values": values}

    def fence():
        live.update(lax.optimization_barrier(dict(live)))

    def swap(name):
        live[name + "_other"] = permute(live[name], OTHER_CORE)

    def work(left, right, state=(), last=False):
        blocks = [live[left[0]], live[right[0]]]
        return attend(live["lists"], live["q"], blocks, (left[1], right[1]), state, last)

    live["q"] = arrange(live.pop("queries"))
    fence()
    live["q"] = exchange(live["q"])
    live["kv"] = arrange(live.pop("keys"), live.pop("values"))
    near = live.pop("near")
    row = lax.axis_index("yh") * 2 + lax.axis_index("zh")
    lists = [row.astype(jnp.int32).reshape(1), near]
    for pairs in (FLIP_Z, FLIP_Y, FLIP_BOTH):
        lists.append(permute(near, pairs))
    live["lists"] = lists
    fence()
    live["kv"] = exchange(live["kv"])
    fence()
    live["left"], live["right"] = permute(live["kv"], RIGHT), permute(live["kv"], LEFT)
    swap("kv")
    late = lax.optimization_barrier((live["w"], live["kv_other"]))[0]
    far, w_other = permute(late, FAR), permute(late, OTHER_CORE)
    state = work(("kv", 0), ("kv_other", 0))
    for at in range(3):
        live["state%d" % at] = state[at]
    fence()
    swap("left")
    swap("right")
    state = work(("left", -1), ("right", 1), [live.pop("state%d" % at) for at in range(3)])
    for at in range(3):
        live["state%d" % at] = state[at]
    live["far"], live["w_other"] = far, w_other
    fence()
    swap("far")
    (live["att"],) = work(("left_other", -1), ("right_other", 1), [live.pop("state%d" % at) for at in range(3)], True)
    fence()
    att = exchange(live["att"])
    yl, c = lax.axis_index("yl"), lax.axis_index("c")
    ids = jnp.stack([2 * yl + c, 2 * yl + 1 - c, 2 * (1 - yl) + c, 2 * (1 - yl) + 1 - c]).astype(jnp.int32)
    return project(ids, att, live["w"], live["w_other"], live["far"], live["far_other"])


def solution(mesh):
    fine = Mesh(mesh.devices.reshape(SIZES), AXES)
    tile, head = ("yh", "zh", "zl", "x"), ("yl", "c")
    placed = (
        P(tile, head, None),
        P(tile, head, None),
        P(tile, head, None),
        P(tile, None),
        P(head, None),
    )
    return jax.shard_map(
        on_device, mesh=fine, in_specs=placed, out_specs=P(tile, head, None), check_vma=False
    )
```
